32 devices in a mesh: row: 4 (over y, x), col: 8 (over z, core).
Axes of the slice: x: 2, y: 2, z: 4, core: 2. Of those that a mesh axis runs over, the one named last changes fastest.
Arguments:
- normals: float32 [2048, 16384], P('row', 'col'), may hold values from -6 to 6
- factor: float32 [16384, 16384], P('row', 'col'), as said below
- cell_entity: int32 [16384], P('row'), may hold values from 0 to 1023
- scale: float32 [16384], P('row'), may hold values from 0.25 to 2
- volatility: float32 [16384], P('row'), may hold values from 0.1 to 0.6
- retention: int32 [16384], P('row'), may hold values from 1 to 11
- limit: int32 [16384], P('row'), may hold values from 1 to 15
Outputs:
- entity_loss: float32 [2, 2048, 1024], P(None, 'col', 'row')
The draws below stay inside these ranges and needn't reach their ends.
Inputs may be any that keep to these rules, and one draw needn't show every extreme that they name: factor is zero above the diagonal and one on it.
All inputs are finite; a program needn't handle non-finite values.
Results may differ from the reference program's by a relative error of at most 0.000078.
Values sent between devices are 32-bit elements; how exact they have to be, the bound alone decides.
A program may use at most 128 MiB of HBM per device.

```python
import math
import jax
import jax.numpy as jnp
from jax import lax

CELLS = 16384
ENT = 1024
SCEN = 2048


def draw_factor(key, part):
    rows = jnp.arange(CELLS, dtype=jnp.int32)[:, None]
    cols = jnp.arange(CELLS, dtype=jnp.int32)[None, :]
    values = jax.random.normal(key, (CELLS, CELLS), jnp.float32) * (2.0 / CELLS ** 0.5)
    lower = jnp.where(cols < rows, values, 0.0)
    return jnp.where(cols == rows, 1.0, lower).astype(jnp.float32)


def plant(drawn, rng, low, high):
    longest = drawn.shape.index(max(drawn.shape))
    spots = []
    for shift in (0, 1):
        where = [jax.random.randint(jax.random.fold_in(rng, axis), (), 0, length) for axis, length in enumerate(drawn.shape)]
        where[longest] = (where[longest] + shift) % drawn.shape[longest]
        spots.append(tuple(where))
    return drawn.at[spots[0]].set(low).at[spots[1]].set(high)


def block_levels(rng, dims, pieces, smallest, largest):
    level, own = 1.0, jax.random.fold_in(rng, 6)
    for dim, blocks in pieces:
        draws = jnp.exp(jax.random.uniform(jax.random.fold_in(own, dim), (blocks,), jnp.float32, smallest / len(pieces), largest / len(pieces)))
        level = level * jnp.repeat(draws, dims[dim] // blocks).reshape([-1 if axis == dim else 1 for axis in range(len(dims))])
    return level


def gaussian(rng, extent, deviation, most, cuts=(), kind=jnp.bfloat16):
    drawn = jax.random.normal(rng, extent, jnp.float32) * deviation
    if len(cuts) > 0:
        drawn = block_levels(rng, extent, cuts, -0.22, 0.18) * drawn
    return jnp.clip(drawn, min=-most, max=most).astype(kind)


def setup_inputs(seed: int = 0) -> dict:
    key_list = jax.random.split(jax.random.key(seed), 8)
    normals = gaussian(key_list[0], (SCEN, CELLS), 1.0, 6.0, ((0, 4), (1, 8)), jnp.float32)
    factor = draw_factor(jax.random.fold_in(key_list[7], 71), 0)
    cell_entity = plant(jax.random.randint(key_list[2], (CELLS,), 0, ENT), jax.random.fold_in(key_list[2], 1), 0, ENT - 1).astype(jnp.int32)
    scale = jnp.clip(jnp.exp(math.log(2.0) - 2.0794415 * jax.random.uniform(key_list[3], (CELLS,), jnp.float32) ** block_levels(key_list[3], (CELLS,), ((0, 4),), -0.2, 0.2)), 0.25, 2.0)
    volatility = jnp.clip(jnp.exp(math.log(0.6) - 1.7917595 * jax.random.uniform(key_list[4], (CELLS,), jnp.float32) ** block_levels(key_list[4], (CELLS,), ((0, 4),), -0.2, 0.2)), 0.1, 0.6)
    retention = plant(jax.random.randint(key_list[5], (CELLS,), 1, 12), jax.random.fold_in(key_list[5], 1), 1, 11).astype(jnp.int32)
    limit = plant(jax.random.randint(key_list[6], (CELLS,), 1, 16), jax.random.fold_in(key_list[6], 1), 1, 15).astype(jnp.int32)
    return {"normals": normals, "factor": factor, "cell_entity": cell_entity, "scale": scale, "volatility": volatility, "retention": retention, "limit": limit}


def reference(normals, factor, cell_entity, scale, volatility, retention, limit):
    norms = lax.optimization_barrier(jnp.sum(factor * factor, axis=1))
    mixed = lax.dot_general(normals, factor, (((1,), (1,)), ((), ())), precision=lax.Precision.HIGHEST, preferred_element_type=jnp.float32)
    correlated = mixed * lax.rsqrt(norms)[None, :]
    ground = scale[None, :] * jnp.exp(volatility[None, :] * correlated)
    floor_level = 0.25 * retention.astype(jnp.float32)
    cover = 0.25 * limit.astype(jnp.float32)
    ceded = jnp.minimum(jnp.maximum(ground - floor_level[None, :], 0.0), cover[None, :])
    net = ground - ceded
    onehot = (cell_entity[:, None] == jnp.arange(ENT, dtype=jnp.int32)[None, :]).astype(jnp.float32)
    stacked = jnp.stack([net, ceded])
    return jnp.einsum('ksc,ce->kse', stacked, onehot, precision=lax.Precision.HIGHEST)
```

```python
import jax
import jax.numpy as jnp
from jax import lax
from jax.sharding import PartitionSpec as P

ENT = 1024
CHUNKS = 4


def body(normals, factor, cell_entity, scale, volatility, retention, limit):
    rows, cols = lax.axis_size("row"), lax.axis_size("col")
    scen, depth = normals.shape
    per_col = scen * rows // cols
    step = per_col // CHUNKS
    blocks = normals.reshape(scen // per_col, CHUNKS, step, depth)
    norms = lax.psum(jnp.sum(factor * factor, axis=1), "col")
    floor_level = 0.25 * retention.astype(jnp.float32)
    cover = 0.25 * limit.astype(jnp.float32)
    gain = volatility * lax.rsqrt(norms)
    onehot = (cell_entity[:, None] == jnp.arange(ENT, dtype=jnp.int32)[None, :]).astype(jnp.float32)
    mixed = []
    for k in range(CHUNKS):
        gathered = lax.all_gather(blocks[:, k].reshape(-1, depth), "row", axis=0, tiled=True)
        partial_sum = lax.dot_general(
            gathered,
            factor,
            (((1,), (1,)), ((), ())),
            precision=lax.Precision.HIGH,
            preferred_element_type=jnp.float32,
        )
        mixed.append(lax.psum_scatter(partial_sum, "col", scatter_dimension=0, tiled=True))
    sums = []
    for part in mixed:
        ground = scale[None, :] * jnp.exp(gain[None, :] * part)
        ceded = jnp.minimum(jnp.maximum(ground - floor_level[None, :], 0.0), cover[None, :])
        net = ground - ceded
        stacked = jnp.stack([net, ceded])
        sums.append(jnp.einsum("ksc,ce->kse", stacked, onehot, precision=lax.Precision.HIGH))
    local_sums = jnp.concatenate(sums, axis=1)
    return lax.psum_scatter(local_sums, "row", scatter_dimension=2, tiled=True)


def solution(mesh):
    return jax.shard_map(
        body,
        mesh=mesh,
        in_specs=(
            P("row", "col"),
            P("row", "col"),
            P("row"),
            P("row"),
            P("row"),
            P("row"),
            P("row"),
        ),
        out_specs=P(None, "col", "row"),
        check_vma=False,
    )
```

```python
import jax
import jax.numpy as jnp
from jax import lax
from jax.sharding import PartitionSpec as P

ENT = 1024
CHUNKS = 2


def body(normals, factor, cell_entity, scale, volatility, retention, limit):
    rows, cols = lax.axis_size("row"), lax.axis_size("col")
    scen, depth = normals.shape
    per_col = scen * rows // cols
    step = per_col // CHUNKS
    blocks = normals.reshape(scen // per_col, CHUNKS, step, depth)
    norms = lax.psum(jnp.sum(factor * factor, axis=1), "col")
    floor_level = 0.25 * retention.astype(jnp.float32)
    cover = 0.25 * limit.astype(jnp.float32)
    gain = volatility * lax.rsqrt(norms)
    onehot = (cell_entity[:, None] == jnp.arange(ENT, dtype=jnp.int32)[None, :]).astype(jnp.float32)
    mixed = []
    for k in range(CHUNKS):
        gathered = lax.all_gather(blocks[:, k].reshape(-1, depth), "row", axis=0, tiled=True)
        partial_sum = lax.dot_general(
            gathered,
            factor,
            (((1,), (1,)), ((), ())),
            precision=lax.Precision.HIGH,
            preferred_element_type=jnp.float32,
        )
        mixed.append(lax.psum_scatter(partial_sum, "col", scatter_dimension=0, tiled=True))
    sums = []
    for part in mixed:
        ground = scale[None, :] * jnp.exp(gain[None, :] * part)
        ceded = jnp.minimum(jnp.maximum(ground - floor_level[None, :], 0.0), cover[None, :])
        net = ground - ceded
        stacked = jnp.stack([net, ceded])
        sums.append(jnp.einsum("ksc,ce->kse", stacked, onehot, precision=lax.Precision.HIGH))
    local_sums = jnp.concatenate(sums, axis=1)
    return lax.psum_scatter(local_sums, "row", scatter_dimension=2, tiled=True)


def solution(mesh):
    return jax.shard_map(
        body,
        mesh=mesh,
        in_specs=(
            P("row", "col"),
            P("row", "col"),
            P("row"),
            P("row"),
            P("row"),
            P("row"),
            P("row"),
        ),
        out_specs=P(None, "col", "row"),
        check_vma=False,
    )
```
